32 devices in a mesh: fsdp: 32 (over z, y, x, core).
Axes of the slice: x: 2, y: 2, z: 4, core: 2. Of those that a mesh axis runs over, the one named last changes fastest.
Arguments:
- tokens: bfloat16 [4096, 768], P('fsdp')
- doc_ids: int32 [4096], P('fsdp'), may hold values from 0 to 3, as said below
- pad_mask: int32 [4096], P('fsdp'), may hold values from 0 to 1, as said below
- qkv_matrix: bfloat16 [768, 2304], P('fsdp'), may hold values from -0.21875 to 0.21875
- query_bias: bfloat16 [768], P('fsdp'), may hold values from -3 to 3
- value_bias: bfloat16 [768], P('fsdp'), may hold values from -3 to 3
- out_matrix: bfloat16 [768, 768], P('fsdp'), may hold values from -1.75 to 1.75
- out_bias: bfloat16 [768], P('fsdp'), may hold values from -3 to 3
- attn_gain: bfloat16 [768], P('fsdp'), may hold values from 0.25 to 1.75
- attn_shift: bfloat16 [768], P('fsdp'), may hold values from -3 to 3
- up_matrix: bfloat16 [768, 3072], P('fsdp'), may hold values from -0.21875 to 0.21875
- up_bias: bfloat16 [3072], P('fsdp'), may hold values from -3 to 3
- down_matrix: bfloat16 [3072, 768], P('fsdp'), may hold values from -0.109375 to 0.109375
- down_bias: bfloat16 [768], P('fsdp'), may hold values from -3 to 3
- ffn_gain: bfloat16 [768], P('fsdp'), may hold values from 0.25 to 1.75
- ffn_shift: bfloat16 [768], P('fsdp'), may hold values from -3 to 3
- cotangent: bfloat16 [4096, 768], P('fsdp'), may hold values from -6 to 6
Outputs:
- layer_out: bfloat16 [4096, 768], P('fsdp')
- token_grad: float32 [4096, 768], P('fsdp')
- grad_qkv: float32 [768, 2304], P('fsdp')
- grad_qbias: float32 [768], P('fsdp')
- grad_vbias: float32 [768], P('fsdp')
- grad_outmat: float32 [768, 768], P('fsdp')
- grad_outbias: float32 [768], P('fsdp')
- grad_gain_one: float32 [768], P('fsdp')
- grad_shift_one: float32 [768], P('fsdp')
- grad_upmat: float32 [768, 3072], P('fsdp')
- grad_upbias: float32 [3072], P('fsdp')
- grad_downmat: float32 [3072, 768], P('fsdp')
- grad_downbias: float32 [768], P('fsdp')
- grad_gain_two: float32 [768], P('fsdp')
- grad_shift_two: float32 [768], P('fsdp')
The draws below stay inside these ranges and needn't reach their ends.
Inputs may be any that keep to these rules, and one draw needn't show every extreme that they name: `doc_ids`: within each block of 128 rows the ids never fall; the first row has 0 and the last 3; rows with one id are one sequence, padding continues the last one. `pad_mask`: within each block of 128 rows the ones come first and number from 32 to 128; some block is all ones and some has exactly 32.
All inputs are finite; a program needn't handle non-finite values.
Results may differ from the reference program's by a relative error of at most 0.01.
Values may be sent and summed in bfloat16 or wider, within the bound.
A program may use at most 192 MiB of HBM per device.

```python
import math
import jax
import jax.numpy as jnp
from jax import lax

D = 768
FF = 3072
HEADS = 12
ROWS_DEV = 128
TOKENS = 4096


def layout_rows(key):
    key = jax.random.fold_in(key, 11)
    blocks = TOKENS // ROWS_DEV
    key_valid, key_order, key_one, key_two, key_three = jax.random.split(key, 5)
    valid = jax.random.randint(key_valid, (blocks,), ROWS_DEV // 4, ROWS_DEV + 1)
    order = jax.random.permutation(key_order, blocks)
    valid = valid.at[order[0]].set(ROWS_DEV).at[order[1]].set(ROWS_DEV // 4)
    third = valid // 3
    first_cut = jax.random.randint(key_one, (blocks,), 1, third + 1)
    second_cut = jax.random.randint(key_two, (blocks,), third + 1, 2 * third + 1)
    third_cut = jax.random.randint(key_three, (blocks,), 2 * third + 1, 3 * third + 1)
    positions = jnp.arange(ROWS_DEV)[None, :]
    docs = (positions >= first_cut[:, None]).astype(jnp.int32) + (positions >= second_cut[:, None]).astype(jnp.int32) + (positions >= third_cut[:, None]).astype(jnp.int32)
    live = (positions < valid[:, None]).astype(jnp.int32)
    return (docs.reshape(TOKENS), live.reshape(TOKENS))


def draw_doc_ids(key, part):
    return layout_rows(key)[0]


def draw_pad_mask(key, part):
    return layout_rows(key)[1]


def draw_tokens(key, part):
    key_base = jax.random.fold_in(jax.random.fold_in(key, 5), 0)
    values = jax.random.normal(key_base, (TOKENS, D), jnp.float32)
    return values.astype(jnp.bfloat16)


def with_spikes(drawn, stream_key, source, target, shards_of, factor):
    def block_of(axis_at):
        return (jnp.arange(drawn.shape[axis_at]) // (drawn.shape[axis_at] // shards_of)).reshape((-1,) + (1,) * (drawn.ndim - 1 - axis_at))

    one_side = jax.random.permutation(stream_key, shards_of)[block_of(target)]
    other_side = (block_of(target) + shards_of // 2) % shards_of
    return jnp.where((block_of(source) == one_side) | (block_of(source) == other_side), factor * drawn, drawn)


def steps_of(key, dims, cuts, smallest, high):
    level = 1.0
    for position, shards_of in cuts:
        heights = jax.random.uniform(jax.random.fold_in(jax.random.fold_in(key, 6), position), (shards_of,), jnp.float32, smallest / len(cuts), high / len(cuts))
        level = level * jnp.repeat(jnp.exp(heights), dims[position] // shards_of).reshape((-1,) + (1,) * (len(dims) - 1 - position))
    return level


def bell_draw(key, shape, width, reach, cuts=(), held_as=jnp.bfloat16):
    level = steps_of(key, shape, cuts, -0.22, 0.18) if cuts else 1.0
    drawn = jax.random.normal(key, shape, jnp.float32) * width * level
    return jnp.minimum(jnp.maximum(drawn, -reach), reach).astype(held_as)


def noise_with(key, shape, width, reach, cuts, heavy, kind=jnp.bfloat16):
    array = width * jax.random.normal(key, shape, jnp.float32)
    if cuts:
        array = array * steps_of(key, shape, cuts, -0.22, 0.18)
    return jnp.clip(with_spikes(array, jax.random.fold_in(key, 3), *heavy), -reach, reach).astype(kind)


def setup_inputs(seed: int = 0) -> dict:
    streams_of = jax.random.split(jax.random.key(seed), 18)
    return {
        "tokens": draw_tokens(jax.random.fold_in(streams_of[17], 71), 0),
        "doc_ids": draw_doc_ids(jax.random.fold_in(streams_of[17], 71), 0),
        "pad_mask": draw_pad_mask(jax.random.fold_in(streams_of[17], 71), 0),
        "qkv_matrix": bell_draw(streams_of[3], (D, 3 * D), D ** -0.5, 0.21875, ((0, 32),)),
        "query_bias": bell_draw(streams_of[4], (D,), 0.5, 3.0, ((0, 32),)),
        "value_bias": bell_draw(streams_of[5], (D,), 0.5, 3.0, ((0, 32),)),
        "out_matrix": bell_draw(streams_of[6], (D, D), (D // 64) ** -0.5, 1.75, ((0, 32),)),
        "out_bias": bell_draw(streams_of[7], (D,), 0.5, 3.0, ((0, 32),)),
        "attn_gain": jnp.clip(1.0 + 0.15 * jax.random.normal(streams_of[8], (D,), jnp.float32), 0.25, 1.75).astype(jnp.bfloat16),
        "attn_shift": bell_draw(streams_of[9], (D,), 0.5, 3.0, ((0, 32),)),
        "up_matrix": bell_draw(streams_of[10], (D, FF), D ** -0.5, 0.21875, ((0, 32),)),
        "up_bias": bell_draw(streams_of[11], (FF,), 0.5, 3.0, ((0, 32),)),
        "down_matrix": bell_draw(streams_of[12], (FF, D), FF ** -0.5, 0.109375, ((0, 32),)),
        "down_bias": bell_draw(streams_of[13], (D,), 0.5, 3.0, ((0, 32),)),
        "ffn_gain": jnp.clip(1.0 + 0.15 * jax.random.normal(streams_of[14], (D,), jnp.float32), 0.25, 1.75).astype(jnp.bfloat16),
        "ffn_shift": bell_draw(streams_of[15], (D,), 0.5, 3.0, ((0, 32),)),
        "cotangent": noise_with(streams_of[16], (TOKENS, D), 1.0, 6.0, ((0, 32),), (0, 1, 32, 2.75)),
    }


norm_eps = 1e-06
root_half = 0.7071067811865476
inv_root_two_pi = 0.3989422804014327

def layer_norm(values, gain, shift):
    centred = values - lax.optimization_barrier(jnp.mean(values, axis=-1, keepdims=True))
    inverse = lax.rsqrt(lax.optimization_barrier(jnp.mean(centred * centred, axis=-1, keepdims=True)) + norm_eps)
    normed = centred * inverse
    return (normed * gain + shift, normed, inverse)

def norm_back(upstream, normed, inverse, gain):
    scaled = upstream * gain
    return inverse * (scaled - lax.optimization_barrier(jnp.mean(scaled, axis=-1, keepdims=True)) - normed * lax.optimization_barrier(jnp.mean(scaled * normed, axis=-1, keepdims=True)))

def block_pass(tokens, doc_ids, pad_mask, cotangent, params):
    qkv_m, qbias, vbias, out_m, out_b, gain_one, shift_one, up_m, up_b, down_m, down_b, gain_two, shift_two = params
    fl = jnp.float32
    row_count, model_width = tokens.shape
    head_size = model_width // HEADS
    score_scale = 1.0 / math.sqrt(head_size)
    zero_part = jnp.zeros((model_width,), fl)
    qkv = jnp.dot(tokens, qkv_m, preferred_element_type=fl)
    qkv = (qkv + jnp.concatenate([qbias.astype(fl), zero_part, vbias.astype(fl)])).astype(jnp.bfloat16)
    query = qkv[:, :model_width].reshape(row_count, HEADS, head_size)
    key_rows = qkv[:, model_width:2 * model_width].reshape(row_count, HEADS, head_size)
    value_rows = qkv[:, 2 * model_width:].reshape(row_count, HEADS, head_size)
    positions = jnp.arange(row_count)
    visible = (doc_ids[:, None] == doc_ids[None, :]) & ((pad_mask[None, :] == 1) | (positions[:, None] == positions[None, :]))
    scores = jnp.einsum('qhd,khd->hqk', query.astype(fl), key_rows.astype(fl)) * score_scale
    scores = jnp.where(visible[None], scores, -1e+30)
    row_max = lax.optimization_barrier(jnp.max(scores, axis=-1, keepdims=True))
    log_total = row_max + jnp.log(lax.optimization_barrier(jnp.sum(jnp.exp(scores - row_max), axis=-1, keepdims=True)))
    probs_f = jnp.exp(scores - log_total)
    probs_b = probs_f.astype(jnp.bfloat16)
    context = jnp.einsum('hqk,khd->qhd', probs_b.astype(fl), value_rows.astype(fl))
    context = context.reshape(row_count, model_width).astype(jnp.bfloat16)
    attn_sum = tokens.astype(fl) + jnp.dot(context, out_m, preferred_element_type=fl) + out_b.astype(fl)
    hidden, normed_one, inverse_one = layer_norm(attn_sum, gain_one.astype(fl), shift_one.astype(fl))
    hidden_b = hidden.astype(jnp.bfloat16)
    pre_act = jnp.dot(hidden_b, up_m, preferred_element_type=fl) + up_b.astype(fl)
    cdf_part = 0.5 * (1.0 + jax.scipy.special.erf(pre_act * root_half))
    pdf_part = jnp.exp(-0.5 * pre_act * pre_act) * inv_root_two_pi
    activation = (pre_act * cdf_part).astype(jnp.bfloat16)
    ffn_sum = hidden + jnp.dot(activation, down_m, preferred_element_type=fl) + down_b.astype(fl)
    normed_out, normed_two, inverse_two = layer_norm(ffn_sum, gain_two.astype(fl), shift_two.astype(fl))
    layer_out = normed_out.astype(jnp.bfloat16)
    upstream = cotangent.astype(fl)
    g_gain_two = lax.optimization_barrier(jnp.sum(upstream * normed_two, axis=0))
    g_shift_two = lax.optimization_barrier(jnp.sum(upstream, axis=0))
    d_ffn = norm_back(upstream, normed_two, inverse_two, gain_two.astype(fl))
    g_down_b = lax.optimization_barrier(jnp.sum(d_ffn, axis=0))
    d_ffn_b = d_ffn.astype(jnp.bfloat16)
    g_down_m = jnp.dot(activation.T, d_ffn_b, preferred_element_type=fl)
    d_act = jnp.dot(d_ffn_b, down_m.T, preferred_element_type=fl)
    d_pre = d_act * (cdf_part + pre_act * pdf_part)
    g_up_b = lax.optimization_barrier(jnp.sum(d_pre, axis=0))
    d_pre_b = d_pre.astype(jnp.bfloat16)
    g_up_m = jnp.dot(hidden_b.T, d_pre_b, preferred_element_type=fl)
    d_hidden = d_ffn + jnp.dot(d_pre_b, up_m.T, preferred_element_type=fl)
    g_gain_one = lax.optimization_barrier(jnp.sum(d_hidden * normed_one, axis=0))
    g_shift_one = lax.optimization_barrier(jnp.sum(d_hidden, axis=0))
    d_attn = norm_back(d_hidden, normed_one, inverse_one, gain_one.astype(fl))
    g_out_b = lax.optimization_barrier(jnp.sum(d_attn, axis=0))
    d_attn_b = d_attn.astype(jnp.bfloat16)
    g_out_m = jnp.dot(context.T, d_attn_b, preferred_element_type=fl)
    d_context = jnp.dot(d_attn_b, out_m.T, preferred_element_type=fl).astype(jnp.bfloat16)
    d_context = d_context.reshape(row_count, HEADS, head_size).astype(fl)
    d_value = jnp.einsum('hqk,qhd->khd', probs_b.astype(fl), d_context)
    d_probs = jnp.einsum('qhd,khd->hqk', d_context, value_rows.astype(fl))
    delta = lax.optimization_barrier(jnp.sum(probs_f * d_probs, axis=-1, keepdims=True))
    d_scores = (probs_f * (d_probs - delta) * score_scale).astype(jnp.bfloat16).astype(fl)
    d_query = jnp.einsum('hqk,khd->qhd', d_scores, key_rows.astype(fl)).reshape(row_count, model_width)
    d_key = jnp.einsum('hqk,qhd->khd', d_scores, query.astype(fl)).reshape(row_count, model_width)
    d_value = d_value.reshape(row_count, model_width)
    g_qbias = lax.optimization_barrier(jnp.sum(d_query, axis=0))
    g_vbias = lax.optimization_barrier(jnp.sum(d_value, axis=0))
    d_qkv = jnp.concatenate([d_query, d_key, d_value], axis=1).astype(jnp.bfloat16)
    g_qkv_m = jnp.dot(tokens.T, d_qkv, preferred_element_type=fl)
    token_grad = d_attn + jnp.dot(d_qkv, qkv_m.T, preferred_element_type=fl)
    grads = (g_qkv_m, g_qbias, g_vbias, g_out_m, g_out_b, g_gain_one, g_shift_one, g_up_m, g_up_b, g_down_m, g_down_b, g_gain_two, g_shift_two)
    return (layer_out, token_grad, grads)

def reference(tokens, doc_ids, pad_mask, qkv_matrix, query_bias, value_bias, out_matrix, out_bias, attn_gain, attn_shift, up_matrix, up_bias, down_matrix, down_bias, ffn_gain, ffn_shift, cotangent):
    params = (qkv_matrix, query_bias, value_bias, out_matrix, out_bias, attn_gain, attn_shift, up_matrix, up_bias, down_matrix, down_bias, ffn_gain, ffn_shift)
    blocks = TOKENS // ROWS_DEV
    inputs = (tokens.reshape(blocks, ROWS_DEV, D), doc_ids.reshape(blocks, ROWS_DEV), pad_mask.reshape(blocks, ROWS_DEV), cotangent.reshape(blocks, ROWS_DEV, D))
    start = tuple((jnp.zeros(p.shape, jnp.float32) for p in params))

    def advance(carry, item):
        layer_out, token_grad, grads = block_pass(item[0], item[1], item[2], item[3], params)
        return (tuple((c + g for c, g in zip(carry, grads))), (layer_out, token_grad))
    totals, (outputs, grads_in) = lax.scan(advance, start, inputs)
    return (outputs.reshape(TOKENS, D), grads_in.reshape(TOKENS, D), totals[0], totals[1], totals[2], totals[3], totals[4], totals[5], totals[6], totals[7], totals[8], totals[9], totals[10], totals[11], totals[12])
```

```python
import functools
import math

import jax
import jax.numpy as jnp
from jax import lax
from jax.experimental import pallas as pl
from jax.experimental.pallas import tpu as pltpu
from jax.sharding import PartitionSpec as P

HEADS = 12
AXIS = "fsdp"
MESH_IDS = pl.DeviceIdType.MESH
BITS = 5
GROUP = 32
CORE, X, Y, Z1, Z2 = 0, 1, 2, 3, 4
SCATTER_ORDERS = (
    (CORE, X, Y, Z2, Z1),
    (CORE, X, Y, Z2, Z1),
    (CORE, Y, X, Z2, Z1),
    (CORE, Z1, Z2, X, Y),
    (CORE, Z1, Z2, X, Y),
)
VMEM_BYTES = 60 * 1024 * 1024


def bits_of(me):
    return [lax.rem(lax.div(me, 1 << b), 2) for b in range(BITS)]


def toggled(me, mine, r):
    for b in range(BITS):
        if r >> b & 1:
            me = me + (1 << b) * (1 - 2 * mine[b])
    return me


def greet(me, mine):
    barrier = pltpu.get_barrier_semaphore()
    for b in range(BITS):
        pl.semaphore_signal(
            barrier, inc=1, device_id=(toggled(me, mine, 1 << b),), device_id_type=MESH_IDS
        )
    pl.semaphore_wait(barrier, BITS)


def gather_kernel(count, *refs):
    shards, wholes = refs[:count], refs[count : 2 * count]
    send_sem, recv_sem, local_sem = refs[2 * count :]
    me = lax.axis_index(AXIS)
    mine = bits_of(me)
    greet(me, mine)

    def move(k, r, b):
        owner = toggled(me, mine, r)
        source = shards[k] if r == 0 else wholes[k].at[owner]
        slot = r | (1 << b)
        return pltpu.make_async_remote_copy(
            src_ref=source,
            dst_ref=wholes[k].at[owner],
            send_sem=send_sem.at[k, slot],
            recv_sem=recv_sem.at[k, slot],
            device_id=(toggled(me, mine, 1 << b),),
            device_id_type=MESH_IDS,
        )

    def landed(k, r):
        here = wholes[k].at[toggled(me, mine, r)]
        pltpu.make_async_remote_copy(
            src_ref=here,
            dst_ref=here,
            send_sem=send_sem.at[k, r],
            recv_sem=recv_sem.at[k, r],
            device_id=(toggled(me, mine, 1),),
            device_id_type=MESH_IDS,
        ).wait_recv()

    orders = [tuple(reversed(SCATTER_ORDERS[k])) for k in range(count)]
    own = [
        pltpu.make_async_copy(shards[k], wholes[k].at[me], local_sem.at[k]) for k in range(count)
    ]
    sent = [[] for _ in range(count)]
    for k in range(count):
        for b in orders[k]:
            copy = move(k, 0, b)
            copy.start()
            sent[k].append(copy)
    for copy in own:
        copy.start()
    have = [[0] for _ in range(count)]
    for step in range(BITS):
        width = 1 << step
        for i in range(width):
            for k in range(count):
                b = orders[k][step]
                r = have[k][i] | (1 << b)
                landed(k, r)
                for later in orders[k][step + 1 :]:
                    copy = move(k, r, later)
                    copy.start()
                    sent[k].append(copy)
        for k in range(count):
            b = orders[k][step]
            have[k] = have[k] + [r | (1 << b) for r in have[k]]
    for k in range(count):
        own[k].wait()
        for copy in sent[k]:
            copy.wait_send()


def gather_all(shards):
    count = len(shards)
    return pl.pallas_call(
        functools.partial(gather_kernel, count),
        out_shape=[jax.ShapeDtypeStruct((GROUP,) + s.shape, s.dtype) for s in shards],
        in_specs=[pl.BlockSpec(memory_space=pl.ANY)] * count,
        out_specs=[pl.BlockSpec(memory_space=pl.ANY)] * count,
        scratch_shapes=[
            pltpu.SemaphoreType.DMA((count, GROUP)),
            pltpu.SemaphoreType.DMA((count, GROUP)),
            pltpu.SemaphoreType.DMA((count,)),
        ],
        compiler_params=pltpu.CompilerParams(collective_id=0, has_side_effects=True),
        name="gather_all",
    )(*shards)


def priority(order, step):
    left = order[step + 1 :]
    blocks = [0]
    for b in reversed(left):
        blocks = [r | (1 << b) for r in blocks] + blocks
    return blocks


def scatter_kernel(count, *refs):
    parts, outs = refs[:count], refs[count : 2 * count]
    landing = refs[2 * count : 3 * count]
    send_sem, recv_sem = refs[3 * count :]
    me = lax.axis_index(AXIS)
    mine = bits_of(me)
    greet(me, mine)

    slot_of = []
    for k in range(count):
        table, used = {}, 0
        for step in range(BITS):
            for r in priority(SCATTER_ORDERS[k], step):
                table[step, r] = used
                used += 1
        slot_of.append(table)

    def held(k, step, r):
        if step < 0:
            return parts[k].at[toggled(me, mine, r)]
        return landing[k].at[slot_of[k][step, r]]

    def move(k, step, r):
        b = SCATTER_ORDERS[k][step]
        slot = slot_of[k][step, r & ~(1 << b)]
        return pltpu.make_async_remote_copy(
            src_ref=held(k, step - 1, r),
            dst_ref=landing[k].at[slot],
            send_sem=send_sem.at[k, slot],
            recv_sem=recv_sem.at[k, slot],
            device_id=(toggled(me, mine, 1 << b),),
            device_id_type=MESH_IDS,
        )

    copies = {}
    for i in range(GROUP // 2):
        for k in range(count):
            order = SCATTER_ORDERS[k]
            r = priority(order, 0)[i]
            copy = move(k, 0, r | (1 << order[0]))
            copy.start()
            copies[k, 0, r] = copy
    for step in range(BITS):
        for i in range(1 << (BITS - 1 - step)):
            for k in range(count):
                order = SCATTER_ORDERS[k]
                r = priority(order, step)[i]
                copies[k, step, r].wait_recv()
                before, now = held(k, step - 1, r), held(k, step, r)
                columns = now.shape[-1]
                last = step == BITS - 1
                tile = min(columns, 768 if now.shape[0] <= 24 else 256)

                def add(j, carry, before=before, now=now, tile=tile, last=last, k=k):
                    at = pl.ds(pl.multiple_of(j * tile, tile), tile)
                    total = now[:, at].astype(jnp.float32) + before[:, at].astype(jnp.float32)
                    if last:
                        outs[k][:, at] = total
                    else:
                        now[:, at] = total.astype(jnp.bfloat16)
                    return carry

                lax.fori_loop(0, columns // tile, add, 0)
                if not last and r >> order[step + 1] & 1:
                    copy = move(k, step + 1, r)
                    copy.start()
                    copies[k, step + 1, r & ~(1 << order[step + 1])] = copy
    for copy in copies.values():
        copy.wait_send()


def scatter_all(parts):
    count = len(parts)
    return pl.pallas_call(
        functools.partial(scatter_kernel, count),
        out_shape=[jax.ShapeDtypeStruct(p.shape[1:], jnp.float32) for p in parts],
        in_specs=[pl.BlockSpec(memory_space=pltpu.VMEM)] * count,
        out_specs=[pl.BlockSpec(memory_space=pltpu.VMEM)] * count,
        scratch_shapes=[pltpu.VMEM((GROUP - 1,) + p.shape[1:], p.dtype) for p in parts]
        + [
            pltpu.SemaphoreType.DMA((count, GROUP)),
            pltpu.SemaphoreType.DMA((count, GROUP)),
        ],
        compiler_params=pltpu.CompilerParams(
            collective_id=1, has_side_effects=True, vmem_limit_bytes=VMEM_BYTES
        ),
        name="scatter_all",
    )(*parts)


norm_eps = 1e-06
root_half = 0.7071067811865476
inv_root_two_pi = 0.3989422804014327


def layer_norm(values, gain, shift):
    centred = values - jnp.mean(values, axis=-1, keepdims=True)
    inverse = lax.rsqrt(jnp.mean(centred * centred, axis=-1, keepdims=True) + norm_eps)
    normed = centred * inverse
    return (normed * gain + shift, normed, inverse)


def norm_back(upstream, normed, inverse, gain):
    scaled = upstream * gain
    return inverse * (
        scaled
        - jnp.mean(scaled, axis=-1, keepdims=True)
        - normed * jnp.mean(scaled * normed, axis=-1, keepdims=True)
    )


def masked_scores(query, key_rows, visible, score_scale):
    scores = (
        jnp.einsum("qhd,khd->hqk", query, key_rows, preferred_element_type=jnp.float32)
        * score_scale
    )
    return jnp.where(visible[None], scores, -1e30)


def grad_rows(left, right):
    return jnp.einsum("ra,rb->ab", left, right, preferred_element_type=jnp.float32)


def local(
    tokens,
    doc_ids,
    pad_mask,
    qkv_matrix,
    query_bias,
    value_bias,
    out_matrix,
    out_bias,
    attn_gain,
    attn_shift,
    up_matrix,
    up_bias,
    down_matrix,
    down_bias,
    ffn_gain,
    ffn_shift,
    cotangent,
):
    fl = jnp.float32
    in_kernels = lax.axis_size(AXIS) == GROUP
    vectors = jnp.concatenate(
        [
            jnp.stack(
                [
                    query_bias,
                    value_bias,
                    out_bias,
                    attn_gain,
                    attn_shift,
                    down_bias,
                    ffn_gain,
                    ffn_shift,
                ],
                axis=1,
            ),
            up_bias.reshape(query_bias.shape[0], -1),
        ],
        axis=1,
    )
    vector_count = vectors.shape[1]
    if in_kernels:
        vectors = jnp.pad(vectors, ((0, 0), (0, 128 - vector_count)))
        wholes = gather_all([qkv_matrix, out_matrix, up_matrix, down_matrix, vectors])
        wholes = [w.reshape((-1, w.shape[-1])) for w in wholes]
    else:
        wholes = [
            lax.all_gather(w, AXIS, axis=0, tiled=True)
            for w in (qkv_matrix, out_matrix, up_matrix, down_matrix, vectors)
        ]
    qkv_full, outm_full, upm_full, downm_full, vectors_full = wholes
    qbias_full, vbias_full, outb_full, gain_one, shift_one, downb_full, gain_two, shift_two = (
        vectors_full[:, j] for j in range(8)
    )
    upb_full = vectors_full[:, 8:vector_count].reshape(-1)
    qkv_back, outm_back, upm_back, downm_back = qkv_full, outm_full, upm_full, downm_full
    gain_one_back, gain_two_back = gain_one, gain_two
    row_count, model_width = tokens.shape
    head_size = model_width // HEADS
    score_scale = 1.0 / math.sqrt(head_size)
    hidden_width = upm_full.shape[1]
    ratio = hidden_width // model_width
    zero_part = jnp.zeros((model_width,), fl)
    qkv = jnp.dot(tokens, qkv_full, preferred_element_type=fl)
    qkv = (qkv + jnp.concatenate([qbias_full.astype(fl), zero_part, vbias_full.astype(fl)])).astype(
        jnp.bfloat16
    )
    query = qkv[:, :model_width].reshape(row_count, HEADS, head_size)
    key_rows = qkv[:, model_width : 2 * model_width].reshape(row_count, HEADS, head_size)
    value_rows = qkv[:, 2 * model_width :].reshape(row_count, HEADS, head_size)
    positions = jnp.arange(row_count)
    visible = (doc_ids[:, None] == doc_ids[None, :]) & (
        (pad_mask[None, :] == 1) | (positions[:, None] == positions[None, :])
    )
    scores = masked_scores(query, key_rows, visible, score_scale)
    row_max = jnp.max(scores, axis=-1, keepdims=True)
    log_total = row_max + jnp.log(jnp.sum(jnp.exp(scores - row_max), axis=-1, keepdims=True))
    probs_b = jnp.exp(scores - log_total).astype(jnp.bfloat16)
    context = jnp.einsum("hqk,khd->qhd", probs_b, value_rows, preferred_element_type=fl)
    context = context.reshape(row_count, model_width).astype(jnp.bfloat16)
    attn_sum = (
        tokens.astype(fl)
        + jnp.dot(context, outm_full, preferred_element_type=fl)
        + outb_full.astype(fl)
    )
    hidden, normed_one, inverse_one = layer_norm(
        attn_sum, gain_one.astype(fl), shift_one.astype(fl)
    )
    hidden_b = hidden.astype(jnp.bfloat16)
    pre_act = jnp.dot(hidden_b, upm_full, preferred_element_type=fl) + upb_full.astype(fl)
    cdf_part = 0.5 * (1.0 + jax.scipy.special.erf(pre_act * root_half))
    pdf_part = jnp.exp(-0.5 * pre_act * pre_act) * inv_root_two_pi
    activation = (pre_act * cdf_part).astype(jnp.bfloat16)
    ffn_sum = (
        hidden + jnp.dot(activation, downm_full, preferred_element_type=fl) + downb_full.astype(fl)
    )
    normed_out, normed_two, inverse_two = layer_norm(
        ffn_sum, gain_two.astype(fl), shift_two.astype(fl)
    )
    layer_out = normed_out.astype(jnp.bfloat16)
    upstream = cotangent.astype(fl)
    g_gain_two = jnp.sum(upstream * normed_two, axis=0)
    g_shift_two = jnp.sum(upstream, axis=0)
    d_ffn = norm_back(upstream, normed_two, inverse_two, gain_two_back.astype(fl))
    g_down_b = jnp.sum(d_ffn, axis=0)
    d_ffn_b = d_ffn.astype(jnp.bfloat16)
    d_act = jnp.einsum("rd,fd->rf", d_ffn_b, downm_back, preferred_element_type=fl)
    d_pre = d_act * (cdf_part + pre_act * pdf_part)
    g_up_b = jnp.sum(d_pre, axis=0)
    d_pre_b = d_pre.astype(jnp.bfloat16)
    d_hidden = d_ffn + jnp.einsum("rf,df->rd", d_pre_b, upm_back, preferred_element_type=fl)
    g_gain_one = jnp.sum(d_hidden * normed_one, axis=0)
    g_shift_one = jnp.sum(d_hidden, axis=0)
    d_attn = norm_back(d_hidden, normed_one, inverse_one, gain_one_back.astype(fl))
    g_out_b = jnp.sum(d_attn, axis=0)
    d_attn_b = d_attn.astype(jnp.bfloat16)
    d_context = jnp.einsum("re,de->rd", d_attn_b, outm_back, preferred_element_type=fl).astype(
        jnp.bfloat16
    )
    d_context = d_context.reshape(row_count, HEADS, head_size)
    again_scores = masked_scores(query, key_rows, visible, score_scale)
    probs_f = jnp.exp(again_scores - log_total)
    again_probs = probs_f.astype(jnp.bfloat16)
    d_value = jnp.einsum("hqk,qhd->khd", again_probs, d_context, preferred_element_type=fl)
    d_probs = jnp.einsum("qhd,khd->hqk", d_context, value_rows, preferred_element_type=fl)
    delta = jnp.sum(probs_f * d_probs, axis=-1, keepdims=True)
    d_scores = (probs_f * (d_probs - delta) * score_scale).astype(jnp.bfloat16)
    d_query = jnp.einsum("hqk,khd->qhd", d_scores, key_rows, preferred_element_type=fl).reshape(
        row_count, model_width
    )
    d_key = jnp.einsum("hqk,qhd->khd", d_scores, query, preferred_element_type=fl).reshape(
        row_count, model_width
    )
    d_value = d_value.reshape(row_count, model_width)
    g_qbias = jnp.sum(d_query, axis=0)
    g_vbias = jnp.sum(d_value, axis=0)
    d_qkv = jnp.concatenate([d_query, d_key, d_value], axis=1).astype(jnp.bfloat16)
    token_grad = d_attn + jnp.einsum("re,de->rd", d_qkv, qkv_back, preferred_element_type=fl)
    sums = jnp.concatenate(
        [
            jnp.stack(
                [
                    g_qbias,
                    g_vbias,
                    g_out_b,
                    g_gain_one,
                    g_shift_one,
                    g_down_b,
                    g_gain_two,
                    g_shift_two,
                ],
                axis=1,
            ),
            g_up_b.reshape(model_width, ratio),
        ],
        axis=1,
    )
    pairs = ((tokens, d_qkv), (context, d_attn_b), (hidden_b, d_pre_b), (activation, d_ffn_b))
    if in_kernels:
        parts = [grad_rows(left, right).astype(jnp.bfloat16) for left, right in pairs]
        parts.append(jnp.pad(sums, ((0, 0), (0, 128 - vector_count))).astype(jnp.bfloat16))
        owned = scatter_all([p.reshape((GROUP, -1, p.shape[1])) for p in parts])
    else:
        owned = [
            lax.psum_scatter(p, AXIS, scatter_dimension=0, tiled=True)
            for p in [grad_rows(left, right) for left, right in pairs] + [sums]
        ]
    grad_qkv, grad_outmat, grad_upmat, grad_downmat, vec = owned
    grad_upbias = vec[:, 8:vector_count].reshape(-1)
    return (
        layer_out,
        token_grad,
        grad_qkv,
        vec[:, 0],
        vec[:, 1],
        grad_outmat,
        vec[:, 2],
        vec[:, 3],
        vec[:, 4],
        grad_upmat,
        grad_upbias,
        grad_downmat,
        vec[:, 5],
        vec[:, 6],
        vec[:, 7],
    )


def solution(mesh):
    placed = (
        P("fsdp", None),
        P("fsdp"),
        P("fsdp"),
        P("fsdp", None),
        P("fsdp"),
        P("fsdp"),
        P("fsdp", None),
        P("fsdp"),
        P("fsdp"),
        P("fsdp"),
        P("fsdp", None),
        P("fsdp"),
        P("fsdp", None),
        P("fsdp"),
        P("fsdp"),
        P("fsdp"),
        P("fsdp", None),
    )
    return jax.shard_map(
        local,
        mesh=mesh,
        in_specs=placed,
        out_specs=(
            P("fsdp", None),
            P("fsdp", None),
            P("fsdp", None),
            P("fsdp"),
            P("fsdp"),
            P("fsdp", None),
            P("fsdp"),
            P("fsdp"),
            P("fsdp"),
            P("fsdp", None),
            P("fsdp"),
            P("fsdp", None),
            P("fsdp"),
            P("fsdp"),
            P("fsdp"),
        ),
        check_vma=False,
    )
```

```python
import functools
import math

import jax
import jax.numpy as jnp
from jax import lax
from jax.experimental import pallas as pl
from jax.experimental.pallas import tpu as pltpu
from jax.sharding import PartitionSpec as P

HEADS = 12
AXIS = "fsdp"
MESH_IDS = pl.DeviceIdType.MESH
BITS = 5
GROUP = 32
CORE, X, Y, Z1, Z2 = 0, 1, 2, 3, 4
SCATTER_ORDERS = (
    (CORE, X, Y, Z1, Z2),
    (CORE, X, Y, Z1, Z2),
    (CORE, Y, X, Z1, Z2),
    (CORE, Z1, Z2, X, Y),
    (CORE, Z1, Z2, X, Y),
)
VMEM_BYTES = 60 * 1024 * 1024


def bits_of(me):
    return [lax.rem(lax.div(me, 1 << b), 2) for b in range(BITS)]


def toggled(me, mine, r):
    for b in range(BITS):
        if r >> b & 1:
            me = me + (1 << b) * (1 - 2 * mine[b])
    return me


def greet(me, mine):
    barrier = pltpu.get_barrier_semaphore()
    for b in range(BITS):
        pl.semaphore_signal(
            barrier, inc=1, device_id=(toggled(me, mine, 1 << b),), device_id_type=MESH_IDS
        )
    pl.semaphore_wait(barrier, BITS)


def gather_kernel(count, *refs):
    shards, wholes = refs[:count], refs[count : 2 * count]
    send_sem, recv_sem, local_sem = refs[2 * count :]
    me = lax.axis_index(AXIS)
    mine = bits_of(me)
    greet(me, mine)

    def move(k, r, b):
        owner = toggled(me, mine, r)
        source = shards[k] if r == 0 else wholes[k].at[owner]
        slot = r | (1 << b)
        return pltpu.make_async_remote_copy(
            src_ref=source,
            dst_ref=wholes[k].at[owner],
            send_sem=send_sem.at[k, slot],
            recv_sem=recv_sem.at[k, slot],
            device_id=(toggled(me, mine, 1 << b),),
            device_id_type=MESH_IDS,
        )

    def landed(k, r):
        here = wholes[k].at[toggled(me, mine, r)]
        pltpu.make_async_remote_copy(
            src_ref=here,
            dst_ref=here,
            send_sem=send_sem.at[k, r],
            recv_sem=recv_sem.at[k, r],
            device_id=(toggled(me, mine, 1),),
            device_id_type=MESH_IDS,
        ).wait_recv()

    orders = [tuple(reversed(SCATTER_ORDERS[k])) for k in range(count)]
    own = [
        pltpu.make_async_copy(shards[k], wholes[k].at[me], local_sem.at[k]) for k in range(count)
    ]
    sent = [[] for _ in range(count)]
    for k in range(count):
        for b in orders[k]:
            copy = move(k, 0, b)
            copy.start()
            sent[k].append(copy)
    for copy in own:
        copy.start()
    have = [[0] for _ in range(count)]
    for step in range(BITS):
        width = 1 << step
        for i in range(width):
            for k in range(count):
                b = orders[k][step]
                r = have[k][i] | (1 << b)
                landed(k, r)
                for later in orders[k][step + 1 :]:
                    copy = move(k, r, later)
                    copy.start()
                    sent[k].append(copy)
        for k in range(count):
            b = orders[k][step]
            have[k] = have[k] + [r | (1 << b) for r in have[k]]
    for k in range(count):
        own[k].wait()
        for copy in sent[k]:
            copy.wait_send()


def gather_all(shards):
    count = len(shards)
    return pl.pallas_call(
        functools.partial(gather_kernel, count),
        out_shape=[jax.ShapeDtypeStruct((GROUP,) + s.shape, s.dtype) for s in shards],
        in_specs=[pl.BlockSpec(memory_space=pl.ANY)] * count,
        out_specs=[pl.BlockSpec(memory_space=pl.ANY)] * count,
        scratch_shapes=[
            pltpu.SemaphoreType.DMA((count, GROUP)),
            pltpu.SemaphoreType.DMA((count, GROUP)),
            pltpu.SemaphoreType.DMA((count,)),
        ],
        compiler_params=pltpu.CompilerParams(collective_id=0, has_side_effects=True),
        name="gather_all",
    )(*shards)


def priority(order, step):
    left = order[step + 1 :]
    blocks = [0]
    for b in reversed(left):
        blocks = [r | (1 << b) for r in blocks] + blocks
    return blocks


def scatter_kernel(count, *refs):
    parts, outs = refs[:count], refs[count : 2 * count]
    landing = refs[2 * count : 3 * count]
    send_sem, recv_sem = refs[3 * count :]
    me = lax.axis_index(AXIS)
    mine = bits_of(me)
    greet(me, mine)

    slot_of = []
    for k in range(count):
        table, used = {}, 0
        for step in range(BITS):
            for r in priority(SCATTER_ORDERS[k], step):
                table[step, r] = used
                used += 1
        slot_of.append(table)

    def held(k, step, r):
        if step < 0:
            return parts[k].at[toggled(me, mine, r)]
        return landing[k].at[slot_of[k][step, r]]

    def move(k, step, r):
        b = SCATTER_ORDERS[k][step]
        slot = slot_of[k][step, r & ~(1 << b)]
        return pltpu.make_async_remote_copy(
            src_ref=held(k, step - 1, r),
            dst_ref=landing[k].at[slot],
            send_sem=send_sem.at[k, slot],
            recv_sem=recv_sem.at[k, slot],
            device_id=(toggled(me, mine, 1 << b),),
            device_id_type=MESH_IDS,
        )

    copies = {}
    for i in range(GROUP // 2):
        for k in range(count):
            order = SCATTER_ORDERS[k]
            r = priority(order, 0)[i]
            copy = move(k, 0, r | (1 << order[0]))
            copy.start()
            copies[k, 0, r] = copy
    for step in range(BITS):
        for i in range(1 << (BITS - 1 - step)):
            for k in range(count):
                order = SCATTER_ORDERS[k]
                r = priority(order, step)[i]
                copies[k, step, r].wait_recv()
                before, now = held(k, step - 1, r), held(k, step, r)
                columns = now.shape[-1]
                last = step == BITS - 1
                tile = min(columns, 768 if now.shape[0] <= 24 else 256)

                def add(j, carry, before=before, now=now, tile=tile, last=last, k=k):
                    at = pl.ds(pl.multiple_of(j * tile, tile), tile)
                    total = now[:, at].astype(jnp.float32) + before[:, at].astype(jnp.float32)
                    if last:
                        outs[k][:, at] = total
                    else:
                        now[:, at] = total.astype(jnp.bfloat16)
                    return carry

                lax.fori_loop(0, columns // tile, add, 0)
                if not last and r >> order[step + 1] & 1:
                    copy = move(k, step + 1, r)
                    copy.start()
                    copies[k, step + 1, r & ~(1 << order[step + 1])] = copy
    for copy in copies.values():
        copy.wait_send()


def scatter_all(parts):
    count = len(parts)
    return pl.pallas_call(
        functools.partial(scatter_kernel, count),
        out_shape=[jax.ShapeDtypeStruct(p.shape[1:], jnp.float32) for p in parts],
        in_specs=[pl.BlockSpec(memory_space=pltpu.VMEM)] * count,
        out_specs=[pl.BlockSpec(memory_space=pltpu.VMEM)] * count,
        scratch_shapes=[pltpu.VMEM((GROUP - 1,) + p.shape[1:], p.dtype) for p in parts]
        + [
            pltpu.SemaphoreType.DMA((count, GROUP)),
            pltpu.SemaphoreType.DMA((count, GROUP)),
        ],
        compiler_params=pltpu.CompilerParams(
            collective_id=1, has_side_effects=True, vmem_limit_bytes=VMEM_BYTES
        ),
        name="scatter_all",
    )(*parts)


norm_eps = 1e-06
root_half = 0.7071067811865476
inv_root_two_pi = 0.3989422804014327


def layer_norm(values, gain, shift):
    centred = values - jnp.mean(values, axis=-1, keepdims=True)
    inverse = lax.rsqrt(jnp.mean(centred * centred, axis=-1, keepdims=True) + norm_eps)
    normed = centred * inverse
    return (normed * gain + shift, normed, inverse)


def norm_back(upstream, normed, inverse, gain):
    scaled = upstream * gain
    return inverse * (
        scaled
        - jnp.mean(scaled, axis=-1, keepdims=True)
        - normed * jnp.mean(scaled * normed, axis=-1, keepdims=True)
    )


def masked_scores(query, key_rows, visible, score_scale):
    scores = (
        jnp.einsum("qhd,khd->hqk", query, key_rows, preferred_element_type=jnp.float32)
        * score_scale
    )
    return jnp.where(visible[None], scores, -1e30)


def vector_rows(vectors):
    rows = [jnp.pad(v, ((0, 0), (0, 128 - v.shape[1]))) for v in vectors]
    rows = rows + [jnp.zeros_like(rows[0])] * (16 - len(rows))
    return jnp.stack(rows, axis=1)


def attention_back_kernel(
    scale, qkv_ref, back_ref, doc_col, doc_row, pad_row, d_qkv_ref, sums_ref
):
    fl = jnp.float32
    rows, width = back_ref.shape
    size = width // HEADS
    across, down, both = ((1,), (0,)), ((0,), (0,)), ((1,), (1,))

    def dot(a, b, over):
        return lax.dot_general(a, b, (over, ((), ())), preferred_element_type=fl)

    square = (rows, rows)
    same = lax.broadcasted_iota(jnp.int32, square, 0) == lax.broadcasted_iota(
        jnp.int32, square, 1
    )
    visible = (doc_col[...] == doc_row[...]) & ((pad_row[...] == 1) | same)
    for pair in range(HEADS // 2):
        results = []
        for h in (2 * pair, 2 * pair + 1):
            query, key_rows, value_rows = (
                qkv_ref[:, part * width + h * size : part * width + (h + 1) * size]
                for part in range(3)
            )
            back = back_ref[:, h * size : (h + 1) * size]
            scores = jnp.where(visible, dot(query, key_rows, both) * scale, -1e30)
            row_max = jnp.max(scores, axis=-1, keepdims=True)
            total = jnp.sum(jnp.exp(scores - row_max), axis=-1, keepdims=True)
            probs = jnp.exp(scores - (row_max + jnp.log(total)))
            d_value = dot(probs.astype(jnp.bfloat16), back, down)
            d_probs = dot(back, value_rows, both)
            delta = jnp.sum(probs * d_probs, axis=-1, keepdims=True)
            d_scores = (probs * (d_probs - delta) * scale).astype(jnp.bfloat16)
            results.append(
                (dot(d_scores, key_rows, across), dot(d_scores, query, down), d_value)
            )
        for part in range(3):
            block = jnp.concatenate([results[0][part], results[1][part]], axis=1)
            at = pair * 2 * size
            d_qkv_ref[:, part * width + at : part * width + at + 2 * size] = block.astype(
                jnp.bfloat16
            )
            if part != 1:
                row = part // 2
                sums_ref[row : row + 1, at : at + 2 * size] = jnp.sum(
                    block, axis=0, keepdims=True
                )


def attention_back(qkv, d_context, doc_ids, pad_mask):
    rows, width = d_context.shape
    return pl.pallas_call(
        functools.partial(attention_back_kernel, 1.0 / math.sqrt(width // HEADS)),
        out_shape=(
            jax.ShapeDtypeStruct(qkv.shape, jnp.bfloat16),
            jax.ShapeDtypeStruct((2, width), jnp.float32),
        ),
        compiler_params=pltpu.CompilerParams(vmem_limit_bytes=24 * 1024 * 1024),
        name="attention_back",
    )(qkv, d_context, doc_ids[:, None], doc_ids[None], pad_mask[None])


def grad_rows(left, right):
    return jnp.einsum("ra,rb->ab", left, right, preferred_element_type=jnp.float32)


def local(
    tokens,
    doc_ids,
    pad_mask,
    qkv_matrix,
    query_bias,
    value_bias,
    out_matrix,
    out_bias,
    attn_gain,
    attn_shift,
    up_matrix,
    up_bias,
    down_matrix,
    down_bias,
    ffn_gain,
    ffn_shift,
    cotangent,
):
    fl = jnp.float32
    in_kernels = lax.axis_size(AXIS) == GROUP
    owned_vectors = (
        query_bias,
        value_bias,
        out_bias,
        attn_gain,
        attn_shift,
        down_bias,
        ffn_gain,
        ffn_shift,
        up_bias,
    )
    vectors = vector_rows([v[None] for v in owned_vectors])[0]
    if in_kernels:
        wholes = gather_all([qkv_matrix, out_matrix, up_matrix, down_matrix, vectors])
        wholes = [w.reshape((-1, w.shape[-1])) for w in wholes]
    else:
        wholes = [
            lax.all_gather(w, AXIS, axis=0, tiled=True)
            for w in (qkv_matrix, out_matrix, up_matrix, down_matrix, vectors)
        ]
    qkv_full, outm_full, upm_full, downm_full, vectors_full = wholes
    vectors_full = vectors_full.reshape((-1,) + vectors.shape)
    (
        qbias_full,
        vbias_full,
        outb_full,
        gain_one,
        shift_one,
        downb_full,
        gain_two,
        shift_two,
        upb_full,
    ) = (vectors_full[:, j, : v.shape[0]].reshape(-1) for j, v in enumerate(owned_vectors))
    qkv_back, outm_back, upm_back, downm_back = qkv_full, outm_full, upm_full, downm_full
    gain_one_back, gain_two_back = gain_one, gain_two
    row_count, model_width = tokens.shape
    head_size = model_width // HEADS
    score_scale = 1.0 / math.sqrt(head_size)
    hidden_width = upm_full.shape[1]
    ratio = hidden_width // model_width
    zero_part = jnp.zeros((model_width,), fl)
    qkv = jnp.dot(tokens, qkv_full, preferred_element_type=fl)
    qkv = (qkv + jnp.concatenate([qbias_full.astype(fl), zero_part, vbias_full.astype(fl)])).astype(
        jnp.bfloat16
    )
    query = qkv[:, :model_width].reshape(row_count, HEADS, head_size)
    key_rows = qkv[:, model_width : 2 * model_width].reshape(row_count, HEADS, head_size)
    value_rows = qkv[:, 2 * model_width :].reshape(row_count, HEADS, head_size)
    positions = jnp.arange(row_count)
    visible = (doc_ids[:, None] == doc_ids[None, :]) & (
        (pad_mask[None, :] == 1) | (positions[:, None] == positions[None, :])
    )
    scores = masked_scores(query, key_rows, visible, score_scale)
    row_max = jnp.max(scores, axis=-1, keepdims=True)
    log_total = row_max + jnp.log(jnp.sum(jnp.exp(scores - row_max), axis=-1, keepdims=True))
    probs_b = jnp.exp(scores - log_total).astype(jnp.bfloat16)
    context = jnp.einsum("hqk,khd->qhd", probs_b, value_rows, preferred_element_type=fl)
    context = context.reshape(row_count, model_width).astype(jnp.bfloat16)
    attn_sum = (
        tokens.astype(fl)
        + jnp.dot(context, outm_full, preferred_element_type=fl)
        + outb_full.astype(fl)
    )
    hidden, normed_one, inverse_one = layer_norm(
        attn_sum, gain_one.astype(fl), shift_one.astype(fl)
    )
    hidden_b = hidden.astype(jnp.bfloat16)
    pre_act = jnp.dot(hidden_b, upm_full, preferred_element_type=fl) + upb_full.astype(fl)
    cdf_part = 0.5 * (1.0 + jax.scipy.special.erf(pre_act * root_half))
    pdf_part = jnp.exp(-0.5 * pre_act * pre_act) * inv_root_two_pi
    activation = (pre_act * cdf_part).astype(jnp.bfloat16)
    ffn_sum = (
        hidden + jnp.dot(activation, downm_full, preferred_element_type=fl) + downb_full.astype(fl)
    )
    normed_out, normed_two, inverse_two = layer_norm(
        ffn_sum, gain_two.astype(fl), shift_two.astype(fl)
    )
    layer_out = normed_out.astype(jnp.bfloat16)
    upstream = cotangent.astype(fl)
    g_gain_two = jnp.sum(upstream * normed_two, axis=0)
    g_shift_two = jnp.sum(upstream, axis=0)
    d_ffn = norm_back(upstream, normed_two, inverse_two, gain_two_back.astype(fl))
    g_down_b = jnp.sum(d_ffn, axis=0)
    d_ffn_b = d_ffn.astype(jnp.bfloat16)
    d_act = jnp.einsum("rd,fd->rf", d_ffn_b, downm_back, preferred_element_type=fl)
    d_pre = d_act * (cdf_part + pre_act * pdf_part)
    g_up_b = jnp.sum(d_pre, axis=0)
    d_pre_b = d_pre.astype(jnp.bfloat16)
    d_hidden = d_ffn + jnp.einsum("rf,df->rd", d_pre_b, upm_back, preferred_element_type=fl)
    g_gain_one = jnp.sum(d_hidden * normed_one, axis=0)
    g_shift_one = jnp.sum(d_hidden, axis=0)
    d_attn = norm_back(d_hidden, normed_one, inverse_one, gain_one_back.astype(fl))
    g_out_b = jnp.sum(d_attn, axis=0)
    d_attn_b = d_attn.astype(jnp.bfloat16)
    d_context = jnp.einsum("re,de->rd", d_attn_b, outm_back, preferred_element_type=fl).astype(
        jnp.bfloat16
    )
    d_qkv, attn_sums = attention_back(qkv, d_context, doc_ids, pad_mask)
    g_qbias, g_vbias = attn_sums[0], attn_sums[1]
    token_grad = d_attn + jnp.einsum("re,de->rd", d_qkv, qkv_back, preferred_element_type=fl)
    sums = vector_rows(
        [
            g.reshape((lax.axis_size(AXIS), -1))
            for g in (
                g_qbias,
                g_vbias,
                g_out_b,
                g_gain_one,
                g_shift_one,
                g_down_b,
                g_gain_two,
                g_shift_two,
                g_up_b,
            )
        ]
    )
    pairs = ((tokens, d_qkv), (context, d_attn_b), (hidden_b, d_pre_b), (activation, d_ffn_b))
    if in_kernels:
        parts = [grad_rows(left, right).astype(jnp.bfloat16) for left, right in pairs]
        parts = [p.reshape((GROUP, -1, p.shape[1])) for p in parts]
        owned = scatter_all(parts + [sums.astype(jnp.bfloat16)])
    else:
        owned = [
            lax.psum_scatter(p, AXIS, scatter_dimension=0, tiled=True)
            for p in [grad_rows(left, right) for left, right in pairs]
            + [sums.reshape((-1, sums.shape[2]))]
        ]
    grad_qkv, grad_outmat, grad_upmat, grad_downmat, vec = owned
    owned_sums = [vec[j, : v.shape[0]] for j, v in enumerate(owned_vectors)]
    return (
        layer_out,
        token_grad,
        grad_qkv,
        owned_sums[0],
        owned_sums[1],
        grad_outmat,
        owned_sums[2],
        owned_sums[3],
        owned_sums[4],
        grad_upmat,
        owned_sums[8],
        grad_downmat,
        owned_sums[5],
        owned_sums[6],
        owned_sums[7],
    )


def solution(mesh):
    placed = (
        P("fsdp", None),
        P("fsdp"),
        P("fsdp"),
        P("fsdp", None),
        P("fsdp"),
        P("fsdp"),
        P("fsdp", None),
        P("fsdp"),
        P("fsdp"),
        P("fsdp"),
        P("fsdp", None),
        P("fsdp"),
        P("fsdp", None),
        P("fsdp"),
        P("fsdp"),
        P("fsdp"),
        P("fsdp", None),
    )
    return jax.shard_map(
        local,
        mesh=mesh,
        in_specs=placed,
        out_specs=(
            P("fsdp", None),
            P("fsdp", None),
            P("fsdp", None),
            P("fsdp"),
            P("fsdp"),
            P("fsdp", None),
            P("fsdp"),
            P("fsdp"),
            P("fsdp"),
            P("fsdp", None),
            P("fsdp"),
            P("fsdp", None),
            P("fsdp"),
            P("fsdp"),
            P("fsdp"),
        ),
        check_vma=False,
    )
```
